32 devices in a mesh: lat: 16 (over z, y, core), wid: 2 (over x).
Axes of the slice: x: 2, y: 2, z: 4, core: 2. Of those that a mesh axis runs over, the one named last changes fastest.
Arguments:
- acts: float32 [1024, 4608], P('lat', 'wid'), may hold values from -6 to 6
- enc_weight: float32 [4608, 8192], P('wid', 'lat'), may hold values from -0.09375 to 0.09375
- enc_bias: float32 [8192], P('lat'), may hold values from -1.5 to 1.5
- thresholds: float32 [8192], P('lat'), may hold values from 0.05 to 0.5
- dec_weight: float32 [8192, 4608], P('lat', 'wid'), may hold values from -0.0625 to 0.0625
- dec_bias: float32 [4608], P('wid'), may hold values from -2.5 to 2.5
Outputs:
- grad_enc: float32 [4608, 8192], P('wid', 'lat')
- grad_enc_bias: float32 [8192], P('lat')
- grad_dec: float32 [8192, 4608], P('lat', 'wid')
- grad_dec_bias: float32 [4608], P('wid')
- loss: float32 [], replicated
The draws below stay inside these ranges and needn't reach their ends.
All inputs are finite; a program needn't handle non-finite values.
Results may differ from the reference program's by a relative error of at most 0.00023.
Values sent between devices are 32-bit elements; how exact they have to be, the bound alone decides.
No kernel may reach another device: no remote copies, remote signals or barrier semaphores. Data moves between devices by JAX's collectives and lax.ppermute only.
A program may use at most 128 MiB of HBM per device.

```python
import math
import jax
import jax.numpy as jnp
from jax import lax

D = 4608
LATENTS = 8192
ROWS = 1024


def levels(stream_key, dims, split, low, top_value):
    factor_of, own = 1.0, jax.random.fold_in(stream_key, 6)
    for position, shards_of in split:
        heights = jnp.exp(jax.random.uniform(jax.random.fold_in(own, position), (shards_of,), jnp.float32, low / len(split), top_value / len(split)))
        factor_of = factor_of * jnp.repeat(heights, dims[position] // shards_of).reshape([-1 if axis == position else 1 for axis in range(len(dims))])
    return factor_of


def gaussian(rng, dims, width, most, split=(), kind=jnp.bfloat16):
    values = jax.random.normal(rng, dims, jnp.float32) * width
    if len(split) > 0:
        values = levels(rng, dims, split, -0.22, 0.18) * values
    return jnp.clip(values, min=-most, max=most).astype(kind)


def setup_inputs(seed: int = 0) -> dict:
    seeds = jax.random.split(jax.random.key(seed), 7)
    return {
        "acts": gaussian(seeds[0], (ROWS, D), 1.0, 6.0, ((0, 16), (1, 2)), jnp.float32),
        "enc_weight": gaussian(seeds[1], (D, LATENTS), D ** -0.5, 0.09375, ((0, 2), (1, 16)), jnp.float32),
        "enc_bias": gaussian(seeds[2], (LATENTS,), 0.3, 1.5, ((0, 16),), jnp.float32),
        "thresholds": jnp.clip(jnp.exp(math.log(0.5) - 2.3025851 * jax.random.uniform(seeds[3], (LATENTS,), jnp.float32) ** levels(seeds[3], (LATENTS,), ((0, 16),), -0.2, 0.2)), 0.05, 0.5),
        "dec_weight": gaussian(seeds[4], (LATENTS, D), LATENTS ** -0.5, 0.0625, ((0, 16), (1, 2)), jnp.float32),
        "dec_bias": gaussian(seeds[5], (D,), 0.5, 2.5, ((0, 2),), jnp.float32),
    }


gate_width = 0.1

def reference(acts, enc_weight, enc_bias, thresholds, dec_weight, dec_bias):
    highest = lax.Precision.HIGHEST
    pre = jnp.dot(acts, enc_weight, precision=highest, preferred_element_type=jnp.float32) + enc_bias[None, :]
    sig = jax.nn.sigmoid((pre - thresholds[None, :]) / gate_width)
    feats = pre * sig
    slope = sig + pre * sig * (1.0 - sig) / gate_width
    err = jnp.dot(feats, dec_weight, precision=highest, preferred_element_type=jnp.float32) + dec_bias[None, :] - acts
    loss = jnp.sum(err * err) / (ROWS * D)
    grad_out = err / jnp.sqrt(jnp.float32(ROWS))
    grad_dec = jnp.dot(feats.T, grad_out, precision=highest, preferred_element_type=jnp.float32)
    grad_dec_bias = lax.optimization_barrier(jnp.sum(grad_out, axis=0))
    dpre = jnp.dot(grad_out, dec_weight.T, precision=highest, preferred_element_type=jnp.float32) * slope
    grad_enc = jnp.dot(acts.T, dpre, precision=highest, preferred_element_type=jnp.float32)
    grad_enc_bias = lax.optimization_barrier(jnp.sum(dpre, axis=0))
    return (grad_enc, grad_enc_bias, grad_dec, grad_dec_bias, loss)
```

```python
import functools
import jax
import jax.numpy as jnp
from jax import lax
from jax.experimental import pallas as pl
from jax.experimental.pallas import tpu as pltpu
from jax.sharding import Mesh, PartitionSpec as P

GATE_WIDTH = 0.1
TILE = 768
EIGHTHS = (2, 2, 2, 2)
SWAP = [(0, 1), (1, 0)]
LATENCY, START = 1.5, 0.8
LIMIT = {"z": 3, "y": 2, "wid": 2, "core": 4}
ROWS_BY_COLS, ROWS_BY_ROWS = ((1,), (0,)), ((1,), (1,))


def split_bf16(x):
    high = x.astype(jnp.bfloat16)
    return high, (x - high.astype(jnp.float32)).astype(jnp.bfloat16)


def stacked_dot(stack, high, low, dims):
    rows = stack.shape[0] // 2

    def part(a, b):
        return lax.dot_general(a, b, (dims, ((), ())), preferred_element_type=jnp.float32)

    both = part(stack[...], high[...])
    return both[:rows] + both[rows:] + part(stack[:rows], low[...])


def fill(stack, *parts):
    rows, at = stack.shape[0] // 2, 0
    for x in parts:
        high, low = split_bf16(x)
        stack[at : at + x.shape[0]] = high
        stack[rows + at : rows + at + x.shape[0]] = low
        at += x.shape[0]


def product_kernel(dims, first, second, own_high, own_low, far_high, far_low, out, stack):
    fill(stack, first[...], second[...])
    latents = out.shape[1] // 2
    out[:, :latents] = stacked_dot(stack, own_high, own_low, dims)
    out[:, latents:] = stacked_dot(stack, far_high, far_low, dims)


PARAMS = pltpu.CompilerParams(vmem_limit_bytes=20 * 1024 * 1024)
COST = pl.CostEstimate(flops=1, bytes_accessed=1, transcendentals=0)


def product(first, second, weights, dims):
    latents = weights[0].shape[0 if dims == ROWS_BY_ROWS else 1]
    depth = first.shape[1]
    rows = first.shape[0] + second.shape[0]
    whole = pl.BlockSpec(memory_space=pltpu.VMEM)
    return pl.pallas_call(
        functools.partial(product_kernel, dims),
        out_shape=jax.ShapeDtypeStruct((rows, 2 * latents), jnp.float32),
        in_specs=[whole] * 6,
        out_specs=whole,
        scratch_shapes=[pltpu.VMEM((2 * rows, depth), jnp.bfloat16)],
        compiler_params=PARAMS,
        cost_estimate=COST,
    )(first, second, *weights)


def gate_kernel(count, *refs):
    parts = refs[:count]
    limits, own_high, own_low, far_high, far_low, slope, feats, sent, near, far, stack = refs[count:]
    latents = own_high.shape[0]

    pre = sum(p[...] for p in parts) + limits[0:1]
    sig = jax.nn.sigmoid((pre - limits[1:2]) / GATE_WIDTH)
    value = pre * sig
    feats[...] = value[:, :latents]
    sent[...] = value[:, latents:]
    slope[...] = sig + pre * sig * (1.0 - sig) / GATE_WIDTH
    fill(stack, value)

    rows, width = near.shape
    tile = TILE if width % TILE == 0 else width
    for at in range(0, width, tile):
        cut = (slice(None), slice(at, at + tile))
        recon = stacked_dot(stack.at[:, :latents], own_high.at[cut], own_low.at[cut], ROWS_BY_COLS)
        recon += stacked_dot(stack.at[:, latents:], far_high.at[cut], far_low.at[cut], ROWS_BY_COLS)
        near[cut] = recon[:rows]
        far[cut] = recon[rows:]


def gate(parts, limits, weights):
    rows, latents = parts[0].shape
    width = weights[0].shape[1]
    whole = pl.BlockSpec(memory_space=pltpu.VMEM)
    slope_shape = jax.ShapeDtypeStruct((rows, latents), jnp.float32)
    feats_shape = jax.ShapeDtypeStruct((rows, latents // 2), jnp.float32)
    half_shape = jax.ShapeDtypeStruct((rows // 2, width), jnp.float32)
    return pl.pallas_call(
        functools.partial(gate_kernel, len(parts)),
        out_shape=(slope_shape, feats_shape, feats_shape, half_shape, half_shape),
        in_specs=[whole] * (len(parts) + 5),
        out_specs=(whole,) * 5,
        scratch_shapes=[pltpu.VMEM((2 * rows, latents), jnp.bfloat16)],
        compiler_params=PARAMS,
        cost_estimate=COST,
    )(*parts, limits, *weights)


def turn_kernel(count, *refs):
    high, low = refs[count:]
    high[...], low[...] = split_bf16(jnp.concatenate([r[...] for r in refs[:count]], axis=0).T)


def turn(*parts):
    rows, columns = sum(p.shape[0] for p in parts), parts[0].shape[1]
    tile = 256 if columns % 256 == 0 else columns
    shape = jax.ShapeDtypeStruct((columns, rows), jnp.bfloat16)
    return pl.pallas_call(
        functools.partial(turn_kernel, len(parts)),
        out_shape=(shape, shape),
        grid=(columns // tile,),
        in_specs=[pl.BlockSpec((p.shape[0], tile), lambda j: (0, j)) for p in parts],
        out_specs=[pl.BlockSpec((tile, rows), lambda j: (j, 0))] * 2,
        compiler_params=PARAMS,
        cost_estimate=COST,
    )(*parts)


def grad_kernel(scale, by_rows, tile, left_high, left_low, *refs):
    *pieces, out, high, low, result, sems = refs

    def fill_right(cut):
        at = 0
        for p in pieces:
            rows = p.shape[0]
            high[at : at + rows], low[at : at + rows] = split_bf16(p[:, cut])
            at += rows

    def part(a, b):
        return jnp.dot(a, b[...], preferred_element_type=jnp.float32)

    copies = []
    for n, at in enumerate(range(0, out.shape[0 if by_rows else 1], tile)):
        cut = slice(at, at + tile)
        rows, columns = (cut, slice(None)) if by_rows else (slice(None), cut)
        if n == 0 or not by_rows:
            fill_right(columns)
        total = part(left_high[rows], high) + part(left_high[rows], low) + part(left_low[rows], high)
        result[rows, columns] = total * scale
        copies.append(pltpu.make_async_copy(result.at[rows, columns], out.at[rows, columns], sems.at[n]))
        copies[-1].start()
    for copy in copies:
        copy.wait()


def grad(left, pieces, scale, by_rows):
    rows, depth = left[0].shape
    columns = pieces[0].shape[1]
    split = rows if by_rows else columns
    tile = TILE if split % TILE == 0 else split
    shape = (rows, columns)
    return pl.pallas_call(
        functools.partial(grad_kernel, scale, by_rows, tile),
        out_shape=jax.ShapeDtypeStruct(shape, jnp.float32),
        in_specs=[pl.BlockSpec(memory_space=pltpu.VMEM)] * (2 + len(pieces)),
        out_specs=pl.BlockSpec(memory_space=pl.ANY),
        scratch_shapes=[pltpu.VMEM((depth, columns if by_rows else tile), jnp.bfloat16)] * 2
        + [pltpu.VMEM(shape, jnp.float32), pltpu.SemaphoreType.DMA((split // tile,))],
        compiler_params=pltpu.CompilerParams(vmem_limit_bytes=24 * 1024 * 1024),
        cost_estimate=COST,
    )(*left, *pieces)


class Step:
    def __init__(self, lane, cost, rank, fn, *deps):
        self.lane, self.cost, self.rank, self.fn, self.deps = lane, cost, rank, fn, deps
        self.value, self.end, self.waited = None, None, False


class Plan:
    def __init__(self):
        self.steps, self.token, self.now = [], jnp.zeros((), jnp.float32), 0.0
        self.free, self.flying = {}, {}

    def add(self, lane, cost, rank, fn, *deps):
        step = Step(lane, cost, rank, fn, *deps)
        self.steps.append(step)
        return step

    def after(self, value):
        value, self.token = lax.optimization_barrier((value, self.token))
        return value

    def hold(self, steps):
        for step, value in zip(steps, self.after([s.value for s in steps])):
            step.value = value

    def wait(self, step):
        if step.lane != "tc" and not step.waited:
            step.value, step.waited = self.after(step.value), True
            self.flying[step.lane].remove(step)

    def ready(self, step):
        return all(d.end is not None and d.end <= self.now for d in step.deps)

    def start(self, step):
        flying = self.flying.setdefault(step.lane, [])
        if len(flying) >= LIMIT[step.lane]:
            if min(f.end for f in flying) > self.now:
                return False
            self.wait(min(flying, key=lambda f: f.end))
        for d in step.deps:
            self.wait(d)
            d.value = self.after(d.value)
        step.value = step.fn(*[d.value for d in step.deps])
        begin = max(self.now, self.free.get(step.lane, 0.0))
        self.free[step.lane] = begin + step.cost
        step.end = begin + step.cost + LATENCY
        flying.append(step)
        self.now += START
        return True

    def compute(self, step):
        for d in step.deps:
            self.wait(d)
        self.hold(step.deps)
        step.value = self.after(step.fn(*[d.value for d in step.deps]))
        self.now += step.cost
        step.end = self.now

    def run(self):
        left = sorted(self.steps, key=lambda s: s.rank)
        while left:
            for step in [s for s in left if s.lane != "tc"]:
                if self.ready(step) and self.start(step):
                    left.remove(step)
            step = next((s for s in left if s.lane == "tc" and self.ready(s)), None)
            if step is not None:
                left.remove(step)
                self.compute(step)
                continue
            ends = [f.end for flying in self.flying.values() for f in flying if f.end > self.now]
            if left and ends:
                self.now = min(ends)


def fold(x):
    while x.shape[0] > 1:
        half = x.shape[0] // 2
        x = x[:half] + x[half:]
    return x[0]


def cat(*xs):
    return jnp.concatenate(xs, axis=0)


def swap(axis):
    return lambda x: lax.ppermute(x, axis, SWAP)


def per_device(wid, long, acts, enc_weight, enc_bias, thresholds, dec_weight, dec_bias):
    lat = 4 * long
    rows_own, width = acts.shape
    latents = enc_weight.shape[1]
    total_rows = rows_own * lat
    scale = 1.0 / jnp.sqrt(jnp.float32(total_rows))
    pieces = [n * rows_own // sum(EIGHTHS) for n in EIGHTHS]
    plan = Plan()

    def shift(by):
        return lambda x: lax.ppermute(x, "z", [(i, (i + by) % long) for i in range(long)])

    def links(rows):
        return 2 * rows * width * 4 / 70e3

    def gather(own, piece, rank):
        slots = [own] + [None] * (long - 1)
        up, down = (own,), (own,)
        for hop in range(1, long // 2 + 1):
            after = up + down if hop > 1 else up
            up = (plan.add("z", links(piece), rank, lambda x, *_: shift(1)(x), *after),)
            slots[hop] = up[0]
            if hop < long - hop:
                after = down + after[:1] if hop > 1 else down
                down = (plan.add("z", links(piece), rank, lambda x, *_: shift(-1)(x), *after),)
                slots[long - hop] = down[0]
        line = plan.add("tc", 1.0, rank, cat, *slots)
        return line, plan.add("y", links(long * piece), rank, swap("y"), line)

    def scatter(recon, piece, rank):
        beside = plan.add("y", links(long * piece), rank, lambda g: swap("y")(g[4]), recon)

        def split(g, y):
            line = g[3] + y
            return tuple(line[d * piece : (d + 1) * piece] for d in range(long))

        line = plan.add("tc", 1.0, rank, split, recon, beside)
        ups, downs = list(range(long // 2, 0, -1)), list(range(long // 2 + 1, long))
        up = down = None
        while ups or downs:
            before = [x for x in (up, down) if x is not None]
            if ups:
                d = ups.pop(0)
                if up is None:
                    src = plan.add("tc", 0.0, rank, lambda s, d=d: s[d], line)
                else:
                    src = plan.add("tc", 0.5, rank, lambda s, t, *_, d=d: s[d] + t, line, up, *before[1:])
                up = plan.add("z", links(piece), rank, shift(-1), src)
            if downs:
                d = downs.pop(0)
                if down is None:
                    src = plan.add("tc", 0.0, rank, lambda s, d=d: s[d], line)
                else:
                    src = plan.add("tc", 0.5, rank, lambda s, t, *_, d=d: s[d] + t, line, down, *before[:1])
                down = plan.add("z", links(piece), rank, shift(1), src)
        return line, up, down

    def sum_wid(part, rank, cost):
        if wid == 2:
            return part, plan.add("wid", cost, rank, swap("wid"), part)
        return (plan.add("tc", 5.0, rank, lambda a: lax.psum(a, "wid"), part),)

    def parts_of(x):
        high = lax.reduce_precision(x, 8, 7)
        return high.astype(jnp.bfloat16), (x - high).astype(jnp.bfloat16)

    def sums(a, b):
        blocks = jnp.concatenate([a, b], axis=0).reshape(lat // 2, -1, width)
        return jnp.sum(blocks, axis=1), jnp.sum(blocks * blocks, axis=1)

    chunks, at = [], 0
    for k, piece in enumerate(pieces):
        chunks.append(plan.add("tc", 0.2, -10.0 + k, lambda a=at, b=at + piece: acts[a:b]))
        at += piece
    enc_own, dec_own = (plan.add("tc", 0.0, -6.0, lambda w=w: w) for w in (enc_weight, dec_weight))
    limits_own = plan.add("tc", 0.2, -6.0, lambda: jnp.stack([enc_bias, thresholds]))
    enc_far = plan.add("core", 8.0, 2.1, swap("core"), enc_own)
    limits_far = plan.add("core", 0.5, 0.2, swap("core"), limits_own)
    dec_far = plan.add("core", 8.0, 6.2, swap("core"), dec_own)
    limits = plan.add("tc", 0.3, 0.4, lambda a, b: jnp.concatenate([a, b], axis=1), limits_own, limits_far)
    enc_parts = [plan.add("tc", 3.0, 1.0, parts_of, enc_own), plan.add("tc", 3.0, 2.5, parts_of, enc_far)]
    dec_parts = [plan.add("tc", 3.0, 4.5, parts_of, dec_own), plan.add("tc", 3.0, 4.5, parts_of, dec_far)]

    def slopes(g, *ps):
        total = sum(ps) * g[0] * scale
        return total[:, :latents], total[:, latents:]

    def half(n):
        return lambda xs: xs[n]

    count = len(pieces)
    totals, biases, gates, rows, rows_far, feats_far = [], [], [], [], [], []
    errs, errs_far, dpres, dpres_far = [], [], [], []
    for k, (own, piece) in enumerate(zip(chunks, pieces)):
        ranks = [2.0 * k - 2.5 * stage for stage in range(5)]
        late = 100.0 + 2.0 * k
        size = piece / 16
        part_cost = 2 * piece * lat * latents * 4 / 70e3
        near, far = gather(own, piece, ranks[0])
        part = plan.add(
            "tc", 3.6, ranks[1], lambda a, b, *w: product(a, b, w[0] + w[1], ROWS_BY_COLS), near, far, *enc_parts
        )
        parts = sum_wid(part, ranks[1], part_cost)
        gated = plan.add("tc", 3.6, ranks[1], lambda l, v, w, *ps: gate(ps, l, v + w), limits, *dec_parts, *parts)
        line, up, down = scatter(gated, piece, ranks[2])
        err = plan.add(
            "tc", 0.8, ranks[3], lambda s, u, d, a: ((s[0] + u) + d) + dec_bias[None, :] - a, line, up, down, own
        )
        err_near, err_far = gather(err, piece, ranks[3])
        back = plan.add(
            "tc", 3.6, ranks[4], lambda a, b, *w: product(a, b, w[0] + w[1], ROWS_BY_ROWS), err_near, err_far, *dec_parts
        )
        total = sum_wid(back, ranks[4], part_cost)
        dpre = plan.add("tc", 0.9, ranks[4], slopes, gated, *total)
        dpre_far = plan.add("core", 0.5 * size, ranks[4], lambda d: swap("core")(d[1]), dpre)

        pair = plan.add("tc", 0.9 * size, late, cat, near, far)
        rows.append(pair)
        rows_far.append(plan.add("core", 2.0 * size, late, swap("core"), pair))
        feats_far.append(plan.add("core", 0.5 * size, late, lambda g: swap("core")(g[2]), gated))
        pair = plan.add("tc", 0.9 * size, late, cat, err_near, err_far)
        errs_far.append(plan.add("core", 2.0 * size, late, swap("core"), pair))
        errs.append(pair)
        gates.append(gated)
        dpres.append(dpre)
        dpres_far.append(dpre_far)
        totals.append(plan.add("tc", 1.0, late + 3, sums, err_near, err_far))
        biases.append(plan.add("tc", 0.6, late + 4, lambda d, f: (jnp.sum(d[0], axis=0), jnp.sum(f, axis=0)), dpre, dpre_far))

    turned_rows = plan.add("tc", 5.0, 300, turn, *rows, *rows_far)
    turned_feats = plan.add(
        "tc", 1.5, 302, lambda *xs: turn(*[x[1] for x in xs[:count]], *xs[count:]), *gates, *feats_far
    )
    dec_sum = plan.add(
        "tc", 8.0, 400, lambda t, *xs: grad(t, xs, total_rows**-0.5, False), turned_feats, *errs, *errs_far
    )
    enc_sum = plan.add(
        "tc", 8.0, 401,
        lambda t, *xs: grad(t, [x[0] for x in xs[:count]] + list(xs[count:]), 1.0, True),
        turned_rows, *dpres, *dpres_far,
    )
    by_block = plan.add("tc", 0.5, 510, lambda *ts: (sum(t[0] for t in ts), sum(t[1] for t in ts)), *totals)

    def reduced(t):
        return jnp.stack([fold(fold(x.reshape(2, long, width).swapaxes(0, 1))) for x in t])

    column_near = plan.add("tc", 1.0, 511, reduced, by_block)
    column_far = plan.add("core", 0.5, 512, swap("core"), column_near)
    column = plan.add("tc", 0.5, 720, lambda a, b: a + b, column_near, column_far)
    square = plan.add("tc", 0.5, 721, lambda c: jnp.sum(c[1], keepdims=True), column)
    squares = [plan.add("tc", 0.3, 950, lambda x, *_: x, q, enc_sum) for q in sum_wid(square, 722, 0.5)]
    plan.run()

    loss = sum(s.value for s in squares)[0] / (total_rows * width * wid) + plan.token
    grad_enc_bias = sum(b.value[0] for b in biases) + sum(b.value[1] for b in biases)
    return enc_sum.value, grad_enc_bias, dec_sum.value, column.value[0] * scale, loss


def solution(mesh):
    lat, wid = mesh.shape["lat"], mesh.shape["wid"]
    long = lat // 4
    if lat == 16:
        dims, names = (long, 2, 2, wid), ("z", "y", "core", "wid")
    else:
        dims, names = (2, long, 2, wid), ("y", "z", "core", "wid")
    split = Mesh(mesh.devices.reshape(dims), names)
    both = names[:3]
    in_specs = (P(both, "wid"), P("wid", both), P(both), P(both), P(both, "wid"), P("wid"))
    out_specs = (P("wid", both), P(both), P(both, "wid"), P("wid"), P())

    def body(*args):
        return per_device(wid, long, *args)

    return jax.shard_map(body, mesh=split, in_specs=in_specs, out_specs=out_specs, check_vma=False)
```

```python
import functools
import jax
import jax.numpy as jnp
from jax import lax
from jax.experimental import pallas as pl
from jax.experimental.pallas import tpu as pltpu
from jax.sharding import Mesh, PartitionSpec as P

GATE_WIDTH = 0.1
TILE = 768
EIGHTHS = (2, 2, 2, 2)
SWAP = [(0, 1), (1, 0)]
LATENCY, START = 1.5, 0.8
LIMIT = {"z": 3, "y": 2, "wid": 2, "core": 4}
ROWS_BY_COLS, ROWS_BY_ROWS = ((1,), (0,)), ((1,), (1,))


def split_bf16(x):
    high = x.astype(jnp.bfloat16)
    return high, (x - high.astype(jnp.float32)).astype(jnp.bfloat16)


def stacked_dot(stack, high, low, dims):
    rows = stack.shape[0] // 2

    def part(a, b):
        return lax.dot_general(a, b, (dims, ((), ())), preferred_element_type=jnp.float32)

    both = part(stack[...], high[...])
    return both[:rows] + both[rows:] + part(stack[:rows], low[...])


def fill(stack, *parts):
    rows, at = stack.shape[0] // 2, 0
    for x in parts:
        high, low = split_bf16(x)
        stack[at : at + x.shape[0]] = high
        stack[rows + at : rows + at + x.shape[0]] = low
        at += x.shape[0]


def product_kernel(dims, slots, first, second, own_high, own_low, far_high, far_low, out, *rest):
    *stats, stack = rest
    fill(stack, first[...], second[...])
    for n, rows in enumerate((first, second) if slots else ()):
        blocks = rows[...].reshape(slots, rows.shape[0] // slots, rows.shape[1])
        stats[0][0, n * slots : (n + 1) * slots] = jnp.sum(blocks, axis=1)
        stats[0][1, n * slots : (n + 1) * slots] = jnp.sum(blocks * blocks, axis=1)
    latents = out.shape[1] // 2
    out[:, :latents] = stacked_dot(stack, own_high, own_low, dims)
    out[:, latents:] = stacked_dot(stack, far_high, far_low, dims)


PARAMS = pltpu.CompilerParams(vmem_limit_bytes=20 * 1024 * 1024)
COST = pl.CostEstimate(flops=1, bytes_accessed=1, transcendentals=0)


def product(first, second, weights, dims, slots=0):
    latents = weights[0].shape[0 if dims == ROWS_BY_ROWS else 1]
    depth = first.shape[1]
    rows = first.shape[0] + second.shape[0]
    whole = pl.BlockSpec(memory_space=pltpu.VMEM)
    shapes = [jax.ShapeDtypeStruct((rows, 2 * latents), jnp.float32)]
    if slots:
        shapes.append(jax.ShapeDtypeStruct((2, 2 * slots, depth), jnp.float32))
    return pl.pallas_call(
        functools.partial(product_kernel, dims, slots),
        out_shape=shapes,
        in_specs=[whole] * 6,
        out_specs=[whole] * len(shapes),
        scratch_shapes=[pltpu.VMEM((2 * rows, depth), jnp.bfloat16)],
        compiler_params=PARAMS,
        cost_estimate=COST,
    )(first, second, *weights)


def gate_kernel(count, *refs):
    parts = refs[:count]
    limits, own_high, own_low, far_high, far_low, slope, feats, sent, near, far, stack = refs[count:]
    latents = own_high.shape[0]

    pre = sum(p[...] for p in parts) + limits[0:1]
    sig = jax.nn.sigmoid((pre - limits[1:2]) / GATE_WIDTH)
    value = pre * sig
    feats[...] = value[:, :latents]
    sent[...] = value[:, latents:]
    slope[...] = sig + pre * sig * (1.0 - sig) / GATE_WIDTH
    fill(stack, value)

    rows, width = near.shape
    tile = TILE if width % TILE == 0 else width
    for at in range(0, width, tile):
        cut = (slice(None), slice(at, at + tile))
        recon = stacked_dot(stack.at[:, :latents], own_high.at[cut], own_low.at[cut], ROWS_BY_COLS)
        recon += stacked_dot(stack.at[:, latents:], far_high.at[cut], far_low.at[cut], ROWS_BY_COLS)
        near[cut] = recon[:rows]
        far[cut] = recon[rows:]


def gate(parts, limits, weights):
    rows, latents = parts[0].shape
    width = weights[0].shape[1]
    whole = pl.BlockSpec(memory_space=pltpu.VMEM)
    slope_shape = jax.ShapeDtypeStruct((rows, latents), jnp.float32)
    feats_shape = jax.ShapeDtypeStruct((rows, latents // 2), jnp.float32)
    half_shape = jax.ShapeDtypeStruct((rows // 2, width), jnp.float32)
    return pl.pallas_call(
        functools.partial(gate_kernel, len(parts)),
        out_shape=(slope_shape, feats_shape, feats_shape, half_shape, half_shape),
        in_specs=[whole] * (len(parts) + 5),
        out_specs=(whole,) * 5,
        scratch_shapes=[pltpu.VMEM((2 * rows, latents), jnp.bfloat16)],
        compiler_params=PARAMS,
        cost_estimate=COST,
    )(*parts, limits, *weights)


def turn_kernel(count, *refs):
    high, low = refs[count:]
    high[...], low[...] = split_bf16(jnp.concatenate([r[...] for r in refs[:count]], axis=0).T)


def turn(*parts):
    rows, columns = sum(p.shape[0] for p in parts), parts[0].shape[1]
    tile = 256 if columns % 256 == 0 else columns
    shape = jax.ShapeDtypeStruct((columns, rows), jnp.bfloat16)
    return pl.pallas_call(
        functools.partial(turn_kernel, len(parts)),
        out_shape=(shape, shape),
        grid=(columns // tile,),
        in_specs=[pl.BlockSpec((p.shape[0], tile), lambda j: (0, j)) for p in parts],
        out_specs=[pl.BlockSpec((tile, rows), lambda j: (j, 0))] * 2,
        compiler_params=PARAMS,
        cost_estimate=COST,
    )(*parts)


def grad_kernel(scale, near_high, near_low, far_high, far_low, *refs):
    *pieces, out, bias, high, low = refs

    @pl.when(pl.program_id(1) == 0)
    def _():
        at = 0
        for p in pieces:
            rows = p.shape[0]
            high[at : at + rows], low[at : at + rows] = split_bf16(p[...])
            at += rows
        bias[...] = sum(jnp.sum(p[...], axis=0, keepdims=True) for p in pieces)

    def part(a, b):
        return jnp.dot(a[...], b, preferred_element_type=jnp.float32)

    half = near_high.shape[1]
    total = part(near_high, high[:half]) + part(far_high, high[half:])
    total += part(near_high, low[:half]) + part(far_high, low[half:])
    total += part(near_low, high[:half]) + part(far_low, high[half:])
    out[...] = total * scale


def grad(near, far, near_pieces, far_pieces, scale, by_rows):
    rows, half = near[0].shape
    pieces = [*near_pieces, *far_pieces]
    columns = pieces[0].shape[1]
    if by_rows:
        tm, tn = TILE if rows % TILE == 0 else rows, columns
    else:
        tm, tn = rows, TILE if columns % TILE == 0 else columns
    return pl.pallas_call(
        functools.partial(grad_kernel, scale),
        out_shape=(
            jax.ShapeDtypeStruct((rows, columns), jnp.float32),
            jax.ShapeDtypeStruct((1, columns), jnp.float32),
        ),
        grid=(columns // tn, rows // tm),
        in_specs=[pl.BlockSpec((tm, half), lambda j, i: (i, 0))] * 4
        + [pl.BlockSpec((p.shape[0], tn), lambda j, i: (0, j)) for p in pieces],
        out_specs=(pl.BlockSpec((tm, tn), lambda j, i: (i, j)), pl.BlockSpec((1, tn), lambda j, i: (0, j))),
        scratch_shapes=[pltpu.VMEM((2 * half, tn), jnp.bfloat16)] * 2,
        compiler_params=pltpu.CompilerParams(vmem_limit_bytes=56 * 1024 * 1024),
        cost_estimate=COST,
    )(*near, *far, *pieces)


class Step:
    def __init__(self, lane, cost, rank, fn, *deps):
        self.lane, self.cost, self.rank, self.fn, self.deps = lane, cost, rank, fn, deps
        self.value, self.end, self.waited = None, None, False


class Plan:
    def __init__(self):
        self.steps, self.token, self.now = [], jnp.zeros((), jnp.float32), 0.0
        self.free, self.flying = {}, {}

    def add(self, lane, cost, rank, fn, *deps):
        step = Step(lane, cost, rank, fn, *deps)
        self.steps.append(step)
        return step

    def after(self, value):
        value, self.token = lax.optimization_barrier((value, self.token))
        return value

    def hold(self, steps):
        for step, value in zip(steps, self.after([s.value for s in steps])):
            step.value = value

    def wait(self, step):
        if step.lane != "tc" and not step.waited:
            step.value, step.waited = self.after(step.value), True
            self.flying[step.lane].remove(step)

    def ready(self, step):
        return all(d.end is not None and d.end <= self.now for d in step.deps)

    def start(self, step):
        flying = self.flying.setdefault(step.lane, [])
        if len(flying) >= LIMIT[step.lane]:
            if min(f.end for f in flying) > self.now:
                return False
            self.wait(min(flying, key=lambda f: f.end))
        for d in step.deps:
            self.wait(d)
            d.value = self.after(d.value)
        step.value = step.fn(*[d.value for d in step.deps])
        begin = max(self.now, self.free.get(step.lane, 0.0))
        self.free[step.lane] = begin + step.cost
        step.end = begin + step.cost + LATENCY
        flying.append(step)
        self.now += START
        return True

    def compute(self, step):
        for d in step.deps:
            self.wait(d)
        self.hold(step.deps)
        step.value = self.after(step.fn(*[d.value for d in step.deps]))
        self.now += step.cost
        step.end = self.now

    def run(self):
        left = sorted(self.steps, key=lambda s: s.rank)
        while left:
            for step in [s for s in left if s.lane != "tc"]:
                if self.ready(step) and self.start(step):
                    left.remove(step)
            step = next((s for s in left if s.lane == "tc" and self.ready(s)), None)
            if step is not None:
                left.remove(step)
                self.compute(step)
                continue
            ends = [f.end for flying in self.flying.values() for f in flying if f.end > self.now]
            if left and ends:
                self.now = min(ends)


def fold(x):
    while x.shape[0] > 1:
        half = x.shape[0] // 2
        x = x[:half] + x[half:]
    return x[0]


def cat(*xs):
    return jnp.concatenate(xs, axis=0)


def swap(axis):
    return lambda x: lax.ppermute(x, axis, SWAP)


def per_device(wid, long, acts, enc_weight, enc_bias, thresholds, dec_weight, dec_bias):
    lat = 4 * long
    rows_own, width = acts.shape
    latents = enc_weight.shape[1]
    total_rows = rows_own * lat
    scale = 1.0 / jnp.sqrt(jnp.float32(total_rows))
    pieces = [n * rows_own // sum(EIGHTHS) for n in EIGHTHS]
    plan = Plan()

    def shift(by):
        return lambda x: lax.ppermute(x, "z", [(i, (i + by) % long) for i in range(long)])

    def links(rows):
        return 2 * rows * width * 4 / 70e3

    def gather(own, piece, rank):
        slots = [own] + [None] * (long - 1)
        up, down = (own,), (own,)
        for hop in range(1, long // 2 + 1):
            after = up + down if hop > 1 else up
            up = (plan.add("z", links(piece), rank, lambda x, *_: shift(1)(x), *after),)
            slots[hop] = up[0]
            if hop < long - hop:
                after = down + after[:1] if hop > 1 else down
                down = (plan.add("z", links(piece), rank, lambda x, *_: shift(-1)(x), *after),)
                slots[long - hop] = down[0]
        line = plan.add("tc", 1.0, rank, cat, *slots)
        return line, plan.add("y", links(long * piece), rank, swap("y"), line)

    def scatter(recon, piece, rank):
        beside = plan.add("y", links(long * piece), rank, lambda g: swap("y")(g[4]), recon)

        def split(g, y):
            line = g[3] + y
            return tuple(line[d * piece : (d + 1) * piece] for d in range(long))

        line = plan.add("tc", 1.0, rank, split, recon, beside)
        ups, downs = list(range(long // 2, 0, -1)), list(range(long // 2 + 1, long))
        up = down = None
        while ups or downs:
            before = [x for x in (up, down) if x is not None]
            if ups:
                d = ups.pop(0)
                if up is None:
                    src = plan.add("tc", 0.0, rank, lambda s, d=d: s[d], line)
                else:
                    src = plan.add("tc", 0.5, rank, lambda s, t, *_, d=d: s[d] + t, line, up, *before[1:])
                up = plan.add("z", links(piece), rank, shift(-1), src)
            if downs:
                d = downs.pop(0)
                if down is None:
                    src = plan.add("tc", 0.0, rank, lambda s, d=d: s[d], line)
                else:
                    src = plan.add("tc", 0.5, rank, lambda s, t, *_, d=d: s[d] + t, line, down, *before[:1])
                down = plan.add("z", links(piece), rank, shift(1), src)
        return line, up, down

    def sum_wid(part, rank, cost):
        if wid == 2:
            return part, plan.add("wid", cost, rank, swap("wid"), part)
        return (plan.add("tc", 5.0, rank, lambda a: lax.psum(a, "wid"), part),)

    def parts_of(x):
        high = lax.reduce_precision(x, 8, 7)
        return high.astype(jnp.bfloat16), (x - high).astype(jnp.bfloat16)

    chunks, at = [], 0
    for k, piece in enumerate(pieces):
        chunks.append(plan.add("tc", 0.2, -10.0 + k, lambda a=at, b=at + piece: acts[a:b]))
        at += piece
    enc_own, dec_own = (plan.add("tc", 0.0, -6.0, lambda w=w: w) for w in (enc_weight, dec_weight))
    limits_own = plan.add("tc", 0.2, -6.0, lambda: jnp.stack([enc_bias, thresholds]))
    enc_far = plan.add("core", 8.0, 2.1, swap("core"), enc_own)
    limits_far = plan.add("core", 0.5, 0.2, swap("core"), limits_own)
    dec_far = plan.add("core", 8.0, 6.2, swap("core"), dec_own)
    limits = plan.add("tc", 0.3, 0.4, lambda a, b: jnp.concatenate([a, b], axis=1), limits_own, limits_far)
    enc_parts = [plan.add("tc", 3.0, 1.0, parts_of, enc_own), plan.add("tc", 3.0, 2.5, parts_of, enc_far)]
    dec_parts = [plan.add("tc", 3.0, 4.5, parts_of, dec_own), plan.add("tc", 3.0, 4.5, parts_of, dec_far)]

    def slopes(g, *ps):
        total = sum(ps) * g[0] * scale
        return total[:, :latents], total[:, latents:]

    def half(n):
        return lambda xs: xs[n]

    totals, gates, rows, rows_far, feats_far = [], [], [], [], []
    errs, errs_far, dpres, dpres_far = [], [], [], []
    for k, (own, piece) in enumerate(zip(chunks, pieces)):
        ranks = [2.0 * k - 2.5 * stage for stage in range(5)]
        late = 100.0 + 2.0 * k
        size = piece / 16
        part_cost = 2 * piece * lat * latents * 4 / 70e3
        near, far = gather(own, piece, ranks[0])
        part = plan.add(
            "tc", 3.6, ranks[1], lambda a, b, *w: product(a, b, w[0] + w[1], ROWS_BY_COLS)[0], near, far, *enc_parts
        )
        parts = sum_wid(part, ranks[1], part_cost)
        gated = plan.add("tc", 3.6, ranks[1], lambda l, v, w, *ps: gate(ps, l, v + w), limits, *dec_parts, *parts)
        line, up, down = scatter(gated, piece, ranks[2])
        err = plan.add(
            "tc", 0.8, ranks[3], lambda s, u, d, a: ((s[0] + u) + d) + dec_bias[None, :] - a, line, up, down, own
        )
        err_near, err_far = gather(err, piece, ranks[3])
        both = plan.add(
            "tc", 3.6, ranks[4], lambda a, b, *w: product(a, b, w[0] + w[1], ROWS_BY_ROWS, long), err_near, err_far, *dec_parts
        )
        back = plan.add("tc", 0.0, ranks[4], lambda x: x[0], both)
        totals.append(both)
        total = sum_wid(back, ranks[4], part_cost)
        dpre = plan.add("tc", 0.9, ranks[4], slopes, gated, *total)
        dpre_far = plan.add("core", 0.5 * size, ranks[4], lambda d: swap("core")(d[1]), dpre)

        pair = plan.add("tc", 0.9 * size, late, cat, near, far)
        rows_far.append(plan.add("core", 2.0 * size, late, swap("core"), pair))
        feats_far.append(plan.add("core", 0.5 * size, late, lambda g: swap("core")(g[2]), gated))
        pair = plan.add("tc", 0.9 * size, late, cat, err_near, err_far)
        errs_far.append(plan.add("core", 2.0 * size, late, swap("core"), pair))
        rows += [near, far]
        errs += [err_near, err_far]
        gates.append(gated)
        dpres.append(dpre)
        dpres_far.append(dpre_far)

    turned = [
        plan.add("tc", 3.5, 300, turn, *rows),
        plan.add("tc", 3.5, 301, turn, *rows_far),
        plan.add("tc", 1.0, 302, lambda *gs: turn(*[g[1] for g in gs]), *gates),
        plan.add("tc", 1.0, 303, turn, *feats_far),
    ]
    count = len(pieces)
    dec_sum = plan.add(
        "tc", 9.0, 400,
        lambda n, f, *xs: grad(n, f, xs[: 2 * count], xs[2 * count :], total_rows**-0.5, False),
        *turned[2:], *errs, *errs_far,
    )
    enc_sum = plan.add(
        "tc", 9.0, 401,
        lambda n, f, *xs: grad(n, f, [x[0] for x in xs[:count]], xs[count:], 1.0, True),
        *turned[:2], *dpres, *dpres_far,
    )
    by_block = plan.add("tc", 0.5, 510, lambda *ts: sum(t[1] for t in ts), *totals)

    def reduced(t):
        return jnp.stack([fold(fold(x.reshape(2, long, width).swapaxes(0, 1))) for x in t])

    column_near = plan.add("tc", 1.0, 511, reduced, by_block)
    column_far = plan.add("core", 0.5, 512, swap("core"), column_near)
    column = plan.add("tc", 0.5, 720, lambda a, b: a + b, column_near, column_far)
    square = plan.add("tc", 0.5, 721, lambda c: jnp.sum(c[1], keepdims=True), column)
    squares = [plan.add("tc", 0.3, 950, lambda x, *_: x, q, enc_sum) for q in sum_wid(square, 722, 0.5)]
    plan.run()

    loss = sum(s.value for s in squares)[0] / (total_rows * width * wid) + plan.token
    grad_enc, grad_enc_bias = enc_sum.value
    return grad_enc, grad_enc_bias[0], dec_sum.value[0], column.value[0] * scale, loss


def solution(mesh):
    lat, wid = mesh.shape["lat"], mesh.shape["wid"]
    long = lat // 4
    if lat == 16:
        dims, names = (long, 2, 2, wid), ("z", "y", "core", "wid")
    else:
        dims, names = (2, long, 2, wid), ("y", "z", "core", "wid")
    split = Mesh(mesh.devices.reshape(dims), names)
    both = names[:3]
    in_specs = (P(both, "wid"), P("wid", both), P(both), P(both), P(both, "wid"), P("wid"))
    out_specs = (P("wid", both), P(both), P(both, "wid"), P("wid"), P())

    def body(*args):
        return per_device(wid, long, *args)

    return jax.shard_map(body, mesh=split, in_specs=in_specs, out_specs=out_specs, check_vma=False)
```

```python
import functools
import jax
import jax.numpy as jnp
from jax import lax
from jax.experimental import pallas as pl
from jax.experimental.pallas import tpu as pltpu
from jax.sharding import Mesh, PartitionSpec as P

GATE_WIDTH = 0.1
TILE = 768
EIGHTHS = (2, 2, 2, 2)
SWAP = [(0, 1), (1, 0)]
LATENCY, START = 1.5, 0.8
LIMIT = {"z": 3, "y": 2, "wid": 2, "core": 4}
ROWS_BY_COLS, ROWS_BY_ROWS = ((1,), (0,)), ((1,), (1,))


def split_bf16(x):
    high = x.astype(jnp.bfloat16)
    return high, (x - high.astype(jnp.float32)).astype(jnp.bfloat16)


def stacked_dot(stack, high, low, dims):
    rows = stack.shape[0] // 2

    def part(a, b):
        return lax.dot_general(a, b, (dims, ((), ())), preferred_element_type=jnp.float32)

    both = part(stack[...], high[...])
    return both[:rows] + both[rows:] + part(stack[:rows], low[...])


def fill(stack, *parts):
    rows, at = stack.shape[0] // 2, 0
    for x in parts:
        high, low = split_bf16(x)
        stack[at : at + x.shape[0]] = high
        stack[rows + at : rows + at + x.shape[0]] = low
        at += x.shape[0]


def product_kernel(dims, slots, first, second, own_high, own_low, far_high, far_low, out, *rest):
    *stats, stack = rest
    fill(stack, first[...], second[...])
    for n, rows in enumerate((first, second) if slots else ()):
        blocks = rows[...].reshape(slots, rows.shape[0] // slots, rows.shape[1])
        stats[0][0, n * slots : (n + 1) * slots] = jnp.sum(blocks, axis=1)
        stats[0][1, n * slots : (n + 1) * slots] = jnp.sum(blocks * blocks, axis=1)
    latents = out.shape[1] // 2
    out[:, :latents] = stacked_dot(stack, own_high, own_low, dims)
    out[:, latents:] = stacked_dot(stack, far_high, far_low, dims)


PARAMS = pltpu.CompilerParams(vmem_limit_bytes=20 * 1024 * 1024)
COST = pl.CostEstimate(flops=1, bytes_accessed=1, transcendentals=0)


def product(first, second, weights, dims, slots=0):
    latents = weights[0].shape[0 if dims == ROWS_BY_ROWS else 1]
    depth = first.shape[1]
    rows = first.shape[0] + second.shape[0]
    whole = pl.BlockSpec(memory_space=pltpu.VMEM)
    shapes = [jax.ShapeDtypeStruct((rows, 2 * latents), jnp.float32)]
    if slots:
        shapes.append(jax.ShapeDtypeStruct((2, 2 * slots, depth), jnp.float32))
    return pl.pallas_call(
        functools.partial(product_kernel, dims, slots),
        out_shape=shapes,
        in_specs=[whole] * 6,
        out_specs=[whole] * len(shapes),
        scratch_shapes=[pltpu.VMEM((2 * rows, depth), jnp.bfloat16)],
        compiler_params=PARAMS,
        cost_estimate=COST,
    )(first, second, *weights)


def gate_kernel(count, *refs):
    parts = refs[:count]
    limits, own_high, own_low, far_high, far_low, slope, feats, sent, near, far, stack = refs[count:]
    latents = own_high.shape[0]

    pre = sum(p[...] for p in parts) + limits[0:1]
    sig = jax.nn.sigmoid((pre - limits[1:2]) / GATE_WIDTH)
    value = pre * sig
    feats[...] = value[:, :latents]
    sent[...] = value[:, latents:]
    slope[...] = sig + pre * sig * (1.0 - sig) / GATE_WIDTH
    fill(stack, value)

    rows, width = near.shape
    tile = TILE if width % TILE == 0 else width
    for at in range(0, width, tile):
        cut = (slice(None), slice(at, at + tile))
        recon = stacked_dot(stack.at[:, :latents], own_high.at[cut], own_low.at[cut], ROWS_BY_COLS)
        recon += stacked_dot(stack.at[:, latents:], far_high.at[cut], far_low.at[cut], ROWS_BY_COLS)
        near[cut] = recon[:rows]
        far[cut] = recon[rows:]


def gate(parts, limits, weights):
    rows, latents = parts[0].shape
    width = weights[0].shape[1]
    whole = pl.BlockSpec(memory_space=pltpu.VMEM)
    slope_shape = jax.ShapeDtypeStruct((rows, latents), jnp.float32)
    feats_shape = jax.ShapeDtypeStruct((rows, latents // 2), jnp.float32)
    half_shape = jax.ShapeDtypeStruct((rows // 2, width), jnp.float32)
    return pl.pallas_call(
        functools.partial(gate_kernel, len(parts)),
        out_shape=(slope_shape, feats_shape, feats_shape, half_shape, half_shape),
        in_specs=[whole] * (len(parts) + 5),
        out_specs=(whole,) * 5,
        scratch_shapes=[pltpu.VMEM((2 * rows, latents), jnp.bfloat16)],
        compiler_params=PARAMS,
        cost_estimate=COST,
    )(*parts, limits, *weights)


def turn_kernel(count, *refs):
    high, low = refs[count:]
    high[...], low[...] = split_bf16(jnp.concatenate([r[...] for r in refs[:count]], axis=0).T)


def turn(*parts):
    rows, columns = sum(p.shape[0] for p in parts), parts[0].shape[1]
    tile = 256 if columns % 256 == 0 else columns
    shape = jax.ShapeDtypeStruct((columns, rows), jnp.bfloat16)
    return pl.pallas_call(
        functools.partial(turn_kernel, len(parts)),
        out_shape=(shape, shape),
        grid=(columns // tile,),
        in_specs=[pl.BlockSpec((p.shape[0], tile), lambda j: (0, j)) for p in parts],
        out_specs=[pl.BlockSpec((tile, rows), lambda j: (j, 0))] * 2,
        compiler_params=PARAMS,
        cost_estimate=COST,
    )(*parts)


def grad_kernel(scale, near_high, near_low, far_high, far_low, *refs):
    *pieces, out, bias, high, low = refs

    @pl.when(pl.program_id(1) == 0)
    def _():
        at = 0
        for p in pieces:
            rows = p.shape[0]
            high[at : at + rows], low[at : at + rows] = split_bf16(p[...])
            at += rows
        bias[...] = sum(jnp.sum(p[...], axis=0, keepdims=True) for p in pieces)

    def part(a, b):
        return jnp.dot(a[...], b, preferred_element_type=jnp.float32)

    half = near_high.shape[1]
    total = part(near_high, high[:half]) + part(far_high, high[half:])
    total += part(near_high, low[:half]) + part(far_high, low[half:])
    total += part(near_low, high[:half]) + part(far_low, high[half:])
    out[...] = total * scale


def grad(near, far, near_pieces, far_pieces, scale, by_rows):
    rows, half = near[0].shape
    pieces = [*near_pieces, *far_pieces]
    columns = pieces[0].shape[1]
    if by_rows:
        tm, tn = TILE // 2 if rows % TILE == 0 else rows, columns
    else:
        tm, tn = rows, TILE // 3 if columns % TILE == 0 else columns
    return pl.pallas_call(
        functools.partial(grad_kernel, scale),
        out_shape=(
            jax.ShapeDtypeStruct((rows, columns), jnp.float32),
            jax.ShapeDtypeStruct((1, columns), jnp.float32),
        ),
        grid=(columns // tn, rows // tm),
        in_specs=[pl.BlockSpec((tm, half), lambda j, i: (i, 0))] * 4
        + [pl.BlockSpec((p.shape[0], tn), lambda j, i: (0, j)) for p in pieces],
        out_specs=(pl.BlockSpec((tm, tn), lambda j, i: (i, j)), pl.BlockSpec((1, tn), lambda j, i: (0, j))),
        scratch_shapes=[pltpu.VMEM((2 * half, tn), jnp.bfloat16)] * 2,
        compiler_params=pltpu.CompilerParams(vmem_limit_bytes=56 * 1024 * 1024),
        cost_estimate=COST,
    )(*near, *far, *pieces)


class Step:
    def __init__(self, lane, cost, rank, fn, *deps):
        self.lane, self.cost, self.rank, self.fn, self.deps = lane, cost, rank, fn, deps
        self.value, self.end, self.waited = None, None, False


class Plan:
    def __init__(self):
        self.steps, self.token, self.now = [], jnp.zeros((), jnp.float32), 0.0
        self.free, self.flying = {}, {}

    def add(self, lane, cost, rank, fn, *deps):
        step = Step(lane, cost, rank, fn, *deps)
        self.steps.append(step)
        return step

    def after(self, value):
        value, self.token = lax.optimization_barrier((value, self.token))
        return value

    def hold(self, steps):
        for step, value in zip(steps, self.after([s.value for s in steps])):
            step.value = value

    def wait(self, step):
        if step.lane != "tc" and not step.waited:
            step.value, step.waited = self.after(step.value), True
            self.flying[step.lane].remove(step)

    def ready(self, step):
        return all(d.end is not None and d.end <= self.now for d in step.deps)

    def start(self, step):
        flying = self.flying.setdefault(step.lane, [])
        if len(flying) >= LIMIT[step.lane]:
            if min(f.end for f in flying) > self.now:
                return False
            self.wait(min(flying, key=lambda f: f.end))
        for d in step.deps:
            self.wait(d)
            d.value = self.after(d.value)
        step.value = step.fn(*[d.value for d in step.deps])
        begin = max(self.now, self.free.get(step.lane, 0.0))
        self.free[step.lane] = begin + step.cost
        step.end = begin + step.cost + LATENCY
        flying.append(step)
        self.now += START
        return True

    def compute(self, step):
        for d in step.deps:
            self.wait(d)
        self.hold(step.deps)
        step.value = self.after(step.fn(*[d.value for d in step.deps]))
        self.now += step.cost
        step.end = self.now

    def run(self):
        left = sorted(self.steps, key=lambda s: s.rank)
        while left:
            for step in [s for s in left if s.lane != "tc"]:
                if self.ready(step) and self.start(step):
                    left.remove(step)
            step = next((s for s in left if s.lane == "tc" and self.ready(s)), None)
            if step is not None:
                left.remove(step)
                self.compute(step)
                continue
            ends = [f.end for flying in self.flying.values() for f in flying if f.end > self.now]
            if left and ends:
                self.now = min(ends)


def fold(x):
    while x.shape[0] > 1:
        half = x.shape[0] // 2
        x = x[:half] + x[half:]
    return x[0]


def cat(*xs):
    return jnp.concatenate(xs, axis=0)


def swap(axis):
    return lambda x: lax.ppermute(x, axis, SWAP)


def per_device(wid, long, acts, enc_weight, enc_bias, thresholds, dec_weight, dec_bias):
    lat = 4 * long
    rows_own, width = acts.shape
    latents = enc_weight.shape[1]
    total_rows = rows_own * lat
    scale = 1.0 / jnp.sqrt(jnp.float32(total_rows))
    pieces = [n * rows_own // sum(EIGHTHS) for n in EIGHTHS]
    plan = Plan()

    def shift(by):
        return lambda x: lax.ppermute(x, "z", [(i, (i + by) % long) for i in range(long)])

    def links(rows):
        return 2 * rows * width * 4 / 70e3

    def gather(own, piece, rank):
        slots = [own] + [None] * (long - 1)
        up, down = (own,), (own,)
        for hop in range(1, long // 2 + 1):
            after = up + down if hop > 1 else up
            up = (plan.add("z", links(piece), rank, lambda x, *_: shift(1)(x), *after),)
            slots[hop] = up[0]
            if hop < long - hop:
                after = down + after[:1] if hop > 1 else down
                down = (plan.add("z", links(piece), rank, lambda x, *_: shift(-1)(x), *after),)
                slots[long - hop] = down[0]
        line = plan.add("tc", 1.0, rank, cat, *slots)
        return line, plan.add("y", links(long * piece), rank, swap("y"), line)

    def scatter(recon, piece, rank):
        beside = plan.add("y", links(long * piece), rank, lambda g: swap("y")(g[4]), recon)

        def split(g, y):
            line = g[3] + y
            return tuple(line[d * piece : (d + 1) * piece] for d in range(long))

        line = plan.add("tc", 1.0, rank, split, recon, beside)
        ups, downs = list(range(long // 2, 0, -1)), list(range(long // 2 + 1, long))
        up = down = None
        while ups or downs:
            before = [x for x in (up, down) if x is not None]
            if ups:
                d = ups.pop(0)
                if up is None:
                    src = plan.add("tc", 0.0, rank, lambda s, d=d: s[d], line)
                else:
                    src = plan.add("tc", 0.5, rank, lambda s, t, *_, d=d: s[d] + t, line, up, *before[1:])
                up = plan.add("z", links(piece), rank, shift(-1), src)
            if downs:
                d = downs.pop(0)
                if down is None:
                    src = plan.add("tc", 0.0, rank, lambda s, d=d: s[d], line)
                else:
                    src = plan.add("tc", 0.5, rank, lambda s, t, *_, d=d: s[d] + t, line, down, *before[:1])
                down = plan.add("z", links(piece), rank, shift(1), src)
        return line, up, down

    def sum_wid(part, rank, cost):
        if wid == 2:
            return part, plan.add("wid", cost, rank, swap("wid"), part)
        return (plan.add("tc", 5.0, rank, lambda a: lax.psum(a, "wid"), part),)

    def parts_of(x):
        high = lax.reduce_precision(x, 8, 7)
        return high.astype(jnp.bfloat16), (x - high).astype(jnp.bfloat16)

    chunks, at = [], 0
    for k, piece in enumerate(pieces):
        chunks.append(plan.add("tc", 0.2, -10.0 + k, lambda a=at, b=at + piece: acts[a:b]))
        at += piece
    enc_own, dec_own = (plan.add("tc", 0.0, -6.0, lambda w=w: w) for w in (enc_weight, dec_weight))
    limits_own = plan.add("tc", 0.2, -6.0, lambda: jnp.stack([enc_bias, thresholds]))
    enc_far = plan.add("core", 8.0, 2.1, swap("core"), enc_own)
    limits_far = plan.add("core", 0.5, 0.2, swap("core"), limits_own)
    dec_far = plan.add("core", 8.0, 6.2, swap("core"), dec_own)
    limits = plan.add("tc", 0.3, 0.4, lambda a, b: jnp.concatenate([a, b], axis=1), limits_own, limits_far)
    enc_parts = [plan.add("tc", 3.0, 1.0, parts_of, enc_own), plan.add("tc", 3.0, 2.5, parts_of, enc_far)]
    dec_parts = [plan.add("tc", 3.0, 4.5, parts_of, dec_own), plan.add("tc", 3.0, 4.5, parts_of, dec_far)]

    def slopes(g, *ps):
        total = sum(ps) * g[0] * scale
        return total[:, :latents], total[:, latents:]

    def half(n):
        return lambda xs: xs[n]

    totals, gates, rows, rows_far, feats_far = [], [], [], [], []
    errs, errs_far, dpres, dpres_far = [], [], [], []
    for k, (own, piece) in enumerate(zip(chunks, pieces)):
        ranks = [2.0 * k - 2.5 * stage for stage in range(5)]
        late = 100.0 + 2.0 * k
        size = piece / 16
        part_cost = 2 * piece * lat * latents * 4 / 70e3
        near, far = gather(own, piece, ranks[0])
        part = plan.add(
            "tc", 3.6, ranks[1], lambda a, b, *w: product(a, b, w[0] + w[1], ROWS_BY_COLS)[0], near, far, *enc_parts
        )
        parts = sum_wid(part, ranks[1], part_cost)
        gated = plan.add("tc", 3.6, ranks[1], lambda l, v, w, *ps: gate(ps, l, v + w), limits, *dec_parts, *parts)
        line, up, down = scatter(gated, piece, ranks[2])
        err = plan.add(
            "tc", 0.8, ranks[3], lambda s, u, d, a: ((s[0] + u) + d) + dec_bias[None, :] - a, line, up, down, own
        )
        err_near, err_far = gather(err, piece, ranks[3])
        both = plan.add(
            "tc", 3.6, ranks[4], lambda a, b, *w: product(a, b, w[0] + w[1], ROWS_BY_ROWS, long), err_near, err_far, *dec_parts
        )
        back = plan.add("tc", 0.0, ranks[4], lambda x: x[0], both)
        totals.append(both)
        total = sum_wid(back, ranks[4], part_cost)
        dpre = plan.add("tc", 0.9, ranks[4], slopes, gated, *total)
        dpre_far = plan.add("core", 0.5 * size, ranks[4], lambda d: swap("core")(d[1]), dpre)

        pair = plan.add("tc", 0.9 * size, late, cat, near, far)
        rows_far.append(plan.add("core", 2.0 * size, late, swap("core"), pair))
        feats_far.append(plan.add("core", 0.5 * size, late, lambda g: swap("core")(g[2]), gated))
        pair = plan.add("tc", 0.9 * size, late, cat, err_near, err_far)
        errs_far.append(plan.add("core", 2.0 * size, late, swap("core"), pair))
        rows += [near, far]
        errs += [err_near, err_far]
        gates.append(gated)
        dpres.append(dpre)
        dpres_far.append(dpre_far)

    turned = [
        plan.add("tc", 3.5, 300, turn, *rows),
        plan.add("tc", 3.5, 301, turn, *rows_far),
        plan.add("tc", 1.0, 302, lambda *gs: turn(*[g[1] for g in gs]), *gates),
        plan.add("tc", 1.0, 303, turn, *feats_far),
    ]
    count = len(pieces)
    dec_sum = plan.add(
        "tc", 9.0, 400,
        lambda n, f, *xs: grad(n, f, xs[: 2 * count], xs[2 * count :], total_rows**-0.5, False),
        *turned[2:], *errs, *errs_far,
    )
    enc_sum = plan.add(
        "tc", 9.0, 401,
        lambda n, f, *xs: grad(n, f, [x[0] for x in xs[:count]], xs[count:], 1.0, True),
        *turned[:2], *dpres, *dpres_far,
    )
    by_block = plan.add("tc", 0.5, 510, lambda *ts: sum(t[1] for t in ts), *totals)

    def reduced(t):
        return jnp.stack([fold(fold(x.reshape(2, long, width).swapaxes(0, 1))) for x in t])

    column_near = plan.add("tc", 1.0, 511, reduced, by_block)
    column_far = plan.add("core", 0.5, 512, swap("core"), column_near)
    column = plan.add("tc", 0.5, 720, lambda a, b: a + b, column_near, column_far)
    square = plan.add("tc", 0.5, 721, lambda c: jnp.sum(c[1], keepdims=True), column)
    squares = [plan.add("tc", 0.3, 950, lambda x, *_: x, q, enc_sum) for q in sum_wid(square, 722, 0.5)]
    plan.run()

    loss = sum(s.value for s in squares)[0] / (total_rows * width * wid) + plan.token
    grad_enc, grad_enc_bias = enc_sum.value
    return grad_enc, grad_enc_bias[0], dec_sum.value[0], column.value[0] * scale, loss


def solution(mesh):
    lat, wid = mesh.shape["lat"], mesh.shape["wid"]
    long = lat // 4
    if lat == 16:
        dims, names = (long, 2, 2, wid), ("z", "y", "core", "wid")
    else:
        dims, names = (2, long, 2, wid), ("y", "z", "core", "wid")
    split = Mesh(mesh.devices.reshape(dims), names)
    both = names[:3]
    in_specs = (P(both, "wid"), P("wid", both), P(both), P(both), P(both, "wid"), P("wid"))
    out_specs = (P("wid", both), P(both), P(both, "wid"), P("wid"), P())

    def body(*args):
        return per_device(wid, long, *args)

    return jax.shard_map(body, mesh=split, in_specs=in_specs, out_specs=out_specs, check_vma=False)
```
